1024 devices in a mesh: grp: 8 (over x, core), blk: 32 (over z), rep: 4 (over y).
Axes of the slice: x: 4, y: 4, z: 32, core: 2. Of those that a mesh axis runs over, the one named last changes fastest.
Arguments:
- tod: float32 [8192, 1024], P(('grp', 'blk', 'rep')), may hold values from -6 to 6
- hit_ids: int32 [256, 32, 8], P(('grp', 'blk')), may hold values from 0 to 255
- sample_slot: int32 [8192, 1024], P(('grp', 'blk', 'rep')), may hold values from 0 to 255
- sample_offset: int32 [8192, 1024], P(('grp', 'blk', 'rep')), may hold values from 0 to 127
- prior: float32 [8192, 9], P(('grp', 'blk', 'rep')), may hold values from 0.5 to 8
Outputs:
- offset_amplitudes_iterate: float32 [8192, 16], P(('grp', 'blk', 'rep'))
- leftover_error: float32 [8192, 16], P(('grp', 'blk', 'rep'))
The draws below stay inside these ranges and needn't reach their ends.
Inputs may be any that keep to these rules, and one draw needn't show every extreme that they name: `hit_ids`: A block of the list at owner o is one of owner o's blocks. `sample_slot`: entry s of a list belongs to owner s // 8.
All inputs are finite; a program needn't handle non-finite values.
Results may differ from the reference program's by a relative error of at most 0.0003.
Values sent between devices are 32-bit elements; how exact they have to be, the bound alone decides.
A program may use at most 32 MiB of HBM per device.

```python
import math
import jax
import jax.numpy as jnp

SAMP = 1024
BL = 64
BLOCK = 128
OWN = 256
K = 8
ITERS = 3
NF = 9
ROWS = 8192
LISTS = 256
HOLDER_COUNT = 32
HITS = 256


def plant(array, stream_key, least, largest):
    longest = array.shape.index(max(array.shape))
    spots = []
    for shift in (0, 1):
        where = [jax.random.randint(jax.random.fold_in(stream_key, axis), (), 0, length) for axis, length in enumerate(array.shape)]
        where[longest] = (where[longest] + shift) % array.shape[longest]
        spots.append(tuple(where))
    return array.at[spots[0]].set(least).at[spots[1]].set(largest)


def block_levels(key, shape, cuts, smallest, high):
    def one(dim, blocks):
        draws = jax.random.uniform(jax.random.fold_in(jax.random.fold_in(key, 6), dim), (blocks,), jnp.float32, smallest / len(cuts), high / len(cuts))
        return jnp.repeat(jnp.exp(draws), shape[dim] // blocks).reshape((-1,) + (1,) * (len(shape) - dim - 1))

    loudness = one(*cuts[0])
    for cut in cuts[1:]:
        loudness = loudness * one(*cut)
    return loudness


def bell_draw(key, dims, deviation, bound, shards=(), held_as=jnp.bfloat16):
    level = block_levels(key, dims, shards, -0.22, 0.18) if shards else 1.0
    entries = jax.random.normal(key, dims, jnp.float32) * deviation * level
    return jnp.minimum(jnp.maximum(entries, -bound), bound).astype(held_as)


def setup_inputs(seed: int = 0) -> dict:
    seeds = jax.random.split(jax.random.key(seed), 6)
    tod = bell_draw(seeds[0], (ROWS, SAMP), 1.0, 6.0, ((0, 1024),), jnp.float32)
    hit_ids = plant(jax.random.randint(seeds[1], (LISTS, HOLDER_COUNT, K), 0, OWN), jax.random.fold_in(seeds[1], 1), 0, OWN - 1).astype(jnp.int32)
    sample_slot = plant(jax.random.randint(seeds[2], (ROWS, SAMP), 0, HITS), jax.random.fold_in(seeds[2], 1), 0, HITS - 1).astype(jnp.int32)
    sample_offset = plant(jax.random.randint(seeds[3], (ROWS, SAMP), 0, BLOCK), jax.random.fold_in(seeds[3], 1), 0, BLOCK - 1).astype(jnp.int32)
    prior = jnp.clip(jnp.exp(math.log(8.0) - 2.7725887 * jax.random.uniform(seeds[4], (ROWS, NF), jnp.float32) ** block_levels(seeds[4], (ROWS, NF), ((0, 1024),), -0.2, 0.2)), 0.5, 8.0)
    return {"tod": tod, "hit_ids": hit_ids, "sample_slot": sample_slot, "sample_offset": sample_offset, "prior": prior}


def pixel_of(hit_ids, sample_slot, sample_offset):
    detector_rows = sample_slot.shape[0]
    list_count = hit_ids.shape[0]
    owner_count = hit_ids.shape[1]
    per_owner = hit_ids.shape[2]
    which_list = jnp.arange(detector_rows, dtype=jnp.int32) // (detector_rows // list_count)
    listing = hit_ids.reshape(list_count, owner_count * per_owner)[which_list]
    in_owner = jnp.take_along_axis(listing, sample_slot, axis=1)
    owner_of = sample_slot // per_owner
    return ((owner_of * OWN + in_owner) * BLOCK + sample_offset).astype(jnp.int32)


def filtered(value_entries, prior):
    spectrum = jnp.fft.rfft(value_entries, axis=1)
    return jnp.fft.irfft(prior * spectrum, n=value_entries.shape[1], axis=1).astype(value_entries.dtype)


def reference(tod, hit_ids, sample_slot, sample_offset, prior):
    pixels = pixel_of(hit_ids, sample_slot, sample_offset)
    total = OWN * hit_ids.shape[1] * BLOCK
    flat_pixels = pixels.reshape(-1)
    hits = jax.ops.segment_sum(jnp.ones_like(tod).reshape(-1), flat_pixels, num_segments=total)
    divisor = jnp.maximum(hits, 1.0)

    def cleaned(signal):
        pixel_averaged = jax.ops.segment_sum(signal.reshape(-1), flat_pixels, num_segments=total) / divisor
        return signal - pixel_averaged[pixels]

    def folded(signal):
        return signal.reshape(signal.shape[0], -1, BL).sum(axis=2)

    def operate(value_entries):
        return folded(cleaned(jnp.repeat(value_entries, BL, axis=1))) + filtered(value_entries, prior)

    source_array = folded(cleaned(tod))
    offset_amplitudes_iterate = jnp.zeros_like(source_array)
    leftover_error = source_array
    image = operate(leftover_error)
    norm_now = jnp.sum(leftover_error * leftover_error)
    curvature = jnp.sum(leftover_error * image)
    descent_factor = norm_now / curvature
    update_course, along = leftover_error, image
    for iteration in range(ITERS):
        offset_amplitudes_iterate = offset_amplitudes_iterate + descent_factor * update_course
        leftover_error = leftover_error - descent_factor * along
        if iteration + 1 < ITERS:
            image = operate(leftover_error)
            following_squared_magnitude = jnp.sum(leftover_error * leftover_error)
            curvature = jnp.sum(leftover_error * image)
            factor = following_squared_magnitude / norm_now
            descent_factor = following_squared_magnitude / (curvature - factor * following_squared_magnitude / descent_factor)
            update_course = leftover_error + factor * update_course
            along = image + factor * along
            norm_now = following_squared_magnitude
    return offset_amplitudes_iterate, leftover_error
```

```python
import functools
import math

import jax
import jax.numpy as jnp
from jax import lax
from jax.experimental import pallas as pl
from jax.experimental.pallas import tpu as pltpu
from jax.sharding import PartitionSpec as P

BL = 64
K = 8
LISTS_HERE = 8
REPS = 4
PLANE = 32
LINE = 32
SHARE = 4
DET = 8
SAMP = 1024
LANES = 128
BASES = 16
TILES = SAMP // LANES
ITERS = 3
F32 = jnp.float32
BF16 = jnp.bfloat16
MESH = pl.DeviceIdType.MESH

IDS, TOD, HITS, FIRST = 0, 1, 2, 3
OUT = 6
BACK = 4


def pieces(value, count):
    parts = []
    for _ in range(count):
        part = value.astype(BF16)
        value = value - part.astype(F32)
        parts.append(part)
    return parts


def lanes_of(shape):
    return lax.broadcasted_iota(jnp.int32, shape, len(shape) - 1)


def kernel(
    ids_ref, tod_ref, slot_ref, off_ref, prior_ref, x_ref, r_ref,
    s_hot, o_hot, id_hot, acc, part, tmp, mt, yrow, tot,
    psend, prec, zsend, zrec, bsend, brec, csend, crec, ssend, srec, tsend, trec,
    ps_sem, pr_sem, zs_sem, zr_sem, bs_sem, br_sem, cs_sem, cr_sem,
    ss_sem, sr_sem, ts_sem, tr_sem,
):
    grp = lax.axis_index("grp")
    blk = lax.axis_index("blk")
    rep = lax.axis_index("rep")
    me = grp * REPS + rep
    chips = LISTS_HERE // 2

    def plane_peer(i):
        dx, dc, dy = i // (2 * REPS), (i // REPS) % 2, i % REPS
        g = ((grp // 2 + dx) % chips) * 2 + (grp % 2 + dc) % 2
        return g, (rep + dy) % REPS

    def line_peer(i):
        return (blk + LINE // 2 + (1 - 2 * (i % 2)) * ((i + 1) // 2)) % LINE

    def plane_send(source, target, send, recv):
        @pl.loop(1, PLANE)
        def _(i):
            g, y = plane_peer(i)
            pltpu.make_async_remote_copy(
                src_ref=source(g, y), dst_ref=target, send_sem=send, recv_sem=recv,
                device_id={"grp": g, "rep": y}, device_id_type=MESH,
            ).start()

    def line_send(source, target, send, recv):
        @pl.loop(0, LINE - 1)
        def _(i):
            z = line_peer(i)
            pltpu.make_async_remote_copy(
                src_ref=source(z), dst_ref=target, send_sem=send, recv_sem=recv,
                device_id={"blk": z}, device_id_type=MESH,
            ).start()

    def arrived(view, sem):
        pltpu.make_async_copy(view, view, sem).wait()

    barrier = pltpu.get_barrier_semaphore()

    @pl.loop(1, PLANE)
    def _(i):
        g, y = plane_peer(i)
        pl.semaphore_signal(barrier, inc=1, device_id={"grp": g, "rep": y}, device_id_type=MESH)

    @pl.loop(0, LINE - 1)
    def _(i):
        pl.semaphore_signal(
            barrier, inc=1, device_id={"blk": line_peer(i)}, device_id_type=MESH
        )

    pl.semaphore_wait(barrier, PLANE + LINE - 2)

    for kh in range(2):
        tile = jnp.broadcast_to(ids_ref[kh : kh + 1, :], (SHARE, LANES))
        psend[IDS, 0, kh * SHARE : (kh + 1) * SHARE, :] = tile
        prec[IDS, me, kh * SHARE : (kh + 1) * SHARE, :] = tile
    plane_send(
        lambda g, y: psend.at[IDS, 0], prec.at[IDS, me], ps_sem.at[IDS], pr_sem.at[IDS]
    )

    @pl.loop(0, DET)
    def _(d):
        slot = slot_ref[pl.ds(d, 1), :]
        place = (slot % K) * LINE + slot // K
        rows = lax.broadcasted_iota(jnp.int32, (LINE * K, SAMP), 0)
        s_hot[d] = jnp.where(rows == place, 1.0, 0.0).astype(BF16)
        rows = lax.broadcasted_iota(jnp.int32, (LANES, SAMP), 0)
        o_hot[d] = jnp.where(rows == off_ref[pl.ds(d, 1), :], 1.0, 0.0).astype(BF16)

    def local_map(first):
        acc[...] = jnp.zeros_like(acc)

        @pl.loop(0, DET)
        def _(d):
            hot = o_hot[d]
            left = []
            for p in (first, first + 1):
                row = part[p, pl.ds(d, 1), :]
                left.append(hot * jnp.broadcast_to(row, (LANES, SAMP)).astype(BF16))
            acc[...] += lax.dot_general(
                jnp.concatenate(left, axis=0), s_hot[d],
                (((1,), (1,)), ((), ())), preferred_element_type=F32,
            )

    def send_map(f, image):
        for g in range(PLANE):
            for kh in range(2):
                psend[f, g, kh * SHARE : (kh + 1) * SHARE, :] = image[
                    g * SHARE : (g + 1) * SHARE, kh * LANES : (kh + 1) * LANES
                ]
        prec[f, me] = psend[f, me]
        plane_send(
            lambda g, y: psend.at[f, g * REPS + y], prec.at[f, me], ps_sem.at[f], pr_sem.at[f]
        )

    def to_owners(f):
        arrived(prec.at[f, pl.ds(0, PLANE - 1)], pr_sem.at[f])
        for l in range(LISTS_HERE):
            total = prec[f, l * REPS]
            for y in range(1, REPS):
                total = total + prec[f, l * REPS + y]
            tmp[l * 8 : l * 8 + 8, :] = total
        half = [
            [tmp[pl.ds(kh * SHARE + j, 8, stride=8), :] for kh in range(2)] for j in range(SHARE)
        ]
        lane = lanes_of((8, LANES))
        groups = []
        for kqh in range(2):
            for j in range(SHARE):
                for kql in range(2):
                    kq = kqh * 2 + kql
                    low = pltpu.roll(half[j][0], (-32 * kq) % LANES, 1)
                    high = pltpu.roll(half[j][1], (32 - 32 * kq) % LANES, 1)
                    groups.append(jnp.where(lane < 32, low, high))
        turned = jnp.transpose(jnp.concatenate(groups, axis=0))
        for kh in range(2):
            zsend[f, kh] = turned[kh * LINE : (kh + 1) * LINE].reshape(LINE, 1, LANES)
        zrec[f, :, blk] = zsend[f, :, blk]
        line_send(
            lambda z: zsend.at[f, :, z], zrec.at[f, :, blk], zs_sem.at[f], zr_sem.at[f]
        )

    def at_owner(f):
        arrived(zrec.at[f, :, pl.ds(0, LINE - 1)], zr_sem.at[f])
        rows = jnp.concatenate(
            [zrec[f, kh].reshape(LINE, LANES) for kh in range(2)], axis=0
        )
        both = jnp.concatenate([rows, pltpu.roll(rows, 64, 1)], axis=0)
        tmp[...] = jnp.transpose(both)[:64]
        return jnp.concatenate(
            [tmp[pl.ds(b, SHARE, stride=16), :] for b in range(16)], axis=1
        )

    def merged(f):
        left = jnp.concatenate(pieces(at_owner(f), 3), axis=0)
        out = lax.dot_general(
            left, id_hot[...], (((1,), (1,)), ((), ())), preferred_element_type=F32
        )
        return out[:SHARE] + out[SHARE : 2 * SHARE] + out[2 * SHARE :]

    def send_back(b, values):
        left = jnp.concatenate(pieces(values, 3), axis=0)
        out = jnp.dot(left, id_hot[...], preferred_element_type=F32)
        out = out[:SHARE] + out[SHARE : 2 * SHARE] + out[2 * SHARE :]
        for c in range(16):
            tmp[pl.ds(c, SHARE, stride=16), :] = out[:, c * LANES : (c + 1) * LANES]
        turned = jnp.transpose(
            jnp.concatenate([tmp[...], jnp.zeros((64, LANES), F32)], axis=0)
        )
        rows = jnp.where(
            lanes_of((64, LANES)) < 64, turned[:64], pltpu.roll(turned[64:], 64, 1)
        )
        for kh in range(2):
            bsend[b, kh] = rows[kh * LINE : (kh + 1) * LINE].reshape(LINE, 1, LANES)
        brec[b, :, blk] = bsend[b, :, blk]
        line_send(
            lambda z: bsend.at[b, :, z], brec.at[b, :, blk], bs_sem.at[b], br_sem.at[b]
        )

    def to_lists(b):
        arrived(brec.at[b, :, pl.ds(0, LINE - 1)], br_sem.at[b])
        rows = jnp.concatenate(
            [brec[b, kh].reshape(LINE, LANES) for kh in range(2)], axis=0
        )
        turned = jnp.transpose(
            jnp.concatenate([rows, jnp.zeros((64, LANES), F32)], axis=0)
        )
        quarter = lanes_of((8, LANES)) // 32
        for j in range(SHARE):
            for kh in range(2):
                tile = jnp.zeros((8, LANES), F32)
                for kq in range(4):
                    start = (kq // 2) * 64 + j * 16 + (kq % 2) * 8
                    moved = pltpu.roll(
                        turned[start : start + 8], (32 * kq - 32 * kh) % LANES, 1
                    )
                    tile = jnp.where(quarter == kq, moved, tile)
                csend[b, pl.ds(kh * SHARE + j, 8, stride=8), :] = tile
        crec[b, me] = csend[b, pl.ds(pl.multiple_of(grp * 8, 8), 8), :]
        plane_send(
            lambda g, y: csend.at[b, pl.ds(pl.multiple_of(g * 8, 8), 8)],
            crec.at[b, me], cs_sem.at[b], cr_sem.at[b],
        )

    def picked(b, count):
        arrived(crec.at[b, pl.ds(0, PLANE - 1)], cr_sem.at[b])
        for kh in range(2):
            for g in range(0, PLANE, 2):
                at = slice(kh * SHARE, (kh + 1) * SHARE)
                rows = jnp.concatenate([crec[b, g, at, :], crec[b, g + 1, at, :]], axis=0)
                acc[g * SHARE : g * SHARE + 8, kh * LANES : (kh + 1) * LANES] = rows
        for p, piece in enumerate(pieces(acc[:LANES, :], count)):
            mt[p * LANES : (p + 1) * LANES, :] = piece

        @pl.loop(0, DET)
        def _(d):
            out = jnp.dot(mt[: count * LANES, :], s_hot[d], preferred_element_type=F32)
            total = out[:LANES]
            for p in range(1, count):
                total = total + out[p * LANES : (p + 1) * LANES]
            yrow[pl.ds(d, 1), :] = jnp.sum(
                total * o_hot[d].astype(F32), axis=0, keepdims=True
            )

        return folded(yrow[...])

    def tiles(value):
        return [value[:, t * LANES : (t + 1) * LANES] for t in range(TILES)]

    def folded(value):
        stacked = jnp.concatenate(tiles(value), axis=0)
        a = lax.broadcasted_iota(jnp.int32, (LANES, LANES), 0) // BL
        b = lanes_of((LANES, LANES)) // BL
        ones = jnp.where(a == b, 1.0, 0.0).astype(BF16)
        left = jnp.concatenate(pieces(stacked, 3), axis=0)
        out = jnp.dot(left, ones, preferred_element_type=F32)
        out = out[:64] + out[64:128] + out[128:]
        return jnp.concatenate([out[t * 8 : t * 8 + 8] for t in range(TILES)], axis=1)

    def smoothed(value):
        here = tiles(value)
        swapped = [pltpu.roll(t, 64, 1) for t in here]
        low = lanes_of((DET, LANES)) < 64
        odd = [jnp.where(low, swapped[t - 1], swapped[t]) for t in range(TILES)]
        spectrum = [
            jnp.broadcast_to(prior_ref[:, f : f + 1], (DET, LANES)) for f in range(BASES // 2 + 1)
        ]
        out = [jnp.zeros((DET, LANES), F32) for _ in range(TILES)]
        for shift in range(BASES):
            weight = jnp.zeros((DET, LANES), F32)
            for f in range(BASES // 2 + 1):
                share = (1.0 if f in (0, BASES // 2) else 2.0) / BASES
                weight = weight + spectrum[f] * (
                    share * math.cos(2.0 * math.pi * ((f * shift) % BASES) / BASES)
                )
            source = odd if shift % 2 else here
            for t in range(TILES):
                out[t] = out[t] + weight * source[(t - shift // 2) % TILES]
        return jnp.concatenate(out, axis=1)

    def lane_sums(value):
        total = functools.reduce(lambda a, b: a + b, tiles(value))
        total = jnp.sum(total, axis=0, keepdims=True)
        return total + pltpu.roll(total, 64, 1)

    for p, piece in enumerate(pieces(tod_ref[...], 3)):
        part[p] = piece.astype(F32)
    part[3] = jnp.ones((DET, SAMP), F32)
    local_map(0)
    held = acc[:LANES, :] + acc[LANES:, :]
    local_map(2)
    send_map(TOD, held + acc[:LANES, :])
    send_map(HITS, acc[LANES:, :])
    to_owners(IDS)
    to_owners(TOD)
    to_owners(HITS)
    ids = at_owner(IDS)[0:1, :].astype(jnp.int32)
    rows = lax.broadcasted_iota(jnp.int32, (256, LINE * LISTS_HERE * K), 0)
    id_hot[...] = jnp.where(rows == ids, 1.0, 0.0).astype(BF16)
    sums = merged(TOD)
    divisor = jnp.maximum(merged(HITS), 1.0)
    send_back(0, sums / divisor)
    source = folded(tod_ref[...])
    to_lists(0)
    residual = source - picked(0, 3)

    def apply(n, value):
        f, b = FIRST + n, 1 + n
        for p, piece in enumerate(pieces(value, 2)):
            part[p] = piece.astype(F32)
        local_map(0)
        send_map(f, acc[:LANES, :] + acc[LANES:, :])
        rest = BL * value + smoothed(value)
        square = lane_sums(value * value) * (1.0 / BL)
        product = lane_sums(value * rest) * (1.0 / BL)
        to_owners(f)
        sums = merged(f)
        binned = sums / divisor
        energy = jnp.sum(sums * binned, axis=0, keepdims=True)
        energy = energy[:, :LANES] + energy[:, LANES:]
        energy = energy + pltpu.roll(energy, 64, 1)
        low = lanes_of((1, LANES)) < 64
        row = jnp.where(low, square, product - energy)
        ssend[n] = row
        srec[n, blk] = row
        line_send(lambda z: ssend.at[n], srec.at[n, blk], ss_sem.at[n], sr_sem.at[n])
        send_back(b, binned)
        arrived(srec.at[n, pl.ds(0, LINE - 1)], sr_sem.at[n])
        row = jnp.sum(srec[n], axis=0)
        tsend[n] = row
        trec[n, me] = row
        plane_send(lambda g, y: tsend.at[n], trec.at[n, me], ts_sem.at[n], tr_sem.at[n])
        to_lists(b)
        image = rest - picked(b, 2)
        arrived(trec.at[n, pl.ds(0, PLANE - 1)], tr_sem.at[n])
        row = jnp.sum(trec[n], axis=0)
        rr = jnp.sum(jnp.where(low, row, 0.0), axis=1, keepdims=True)
        curve = jnp.sum(jnp.where(low, 0.0, row), axis=1, keepdims=True)
        return image, rr, curve

    iterate = jnp.zeros((DET, SAMP), F32)
    image, rr, curve = apply(0, residual)
    step = rr / curve
    direction, along = residual, image
    for it in range(ITERS):
        iterate = iterate + step * direction
        residual = residual - step * along
        if it + 1 < ITERS:
            image, new, curve = apply(it + 1, residual)
            ratio = new / rr
            step = new / (curve - ratio * new / step)
            direction = residual + ratio * direction
            along = image + ratio * along
            rr = new

    for ref, value in ((x_ref, iterate), (r_ref, residual)):
        out = jnp.zeros((DET, LANES), F32)
        lane = lanes_of((DET, LANES))
        for t, tile in enumerate(tiles(value)):
            for side in range(2):
                spread = jnp.broadcast_to(tile[:, side * BL : side * BL + 1], (DET, LANES))
                out = jnp.where(lane == 2 * t + side, spread, out)
        ref[...] = out[:, :BASES]

    for f in range(OUT):
        arrived(prec.at[f, pl.ds(0, PLANE - 1)], ps_sem.at[f])
        arrived(zrec.at[f, :, pl.ds(0, LINE - 1)], zs_sem.at[f])
    for b in range(BACK):
        arrived(brec.at[b, :, pl.ds(0, LINE - 1)], bs_sem.at[b])
        arrived(crec.at[b, pl.ds(0, PLANE - 1)], cs_sem.at[b])
    for n in range(ITERS):
        arrived(srec.at[n, pl.ds(0, LINE - 1)], ss_sem.at[n])
        arrived(trec.at[n, pl.ds(0, PLANE - 1)], ts_sem.at[n])


def shards(tod, hit_ids, sample_slot, sample_offset, prior):
    ids = hit_ids[0].T.reshape(2, LANES).astype(F32) * 0.25
    whole = pl.BlockSpec(memory_space=pltpu.VMEM)
    dma = pltpu.SemaphoreType.DMA
    return pl.pallas_call(
        kernel,
        out_shape=[jax.ShapeDtypeStruct((DET, BASES), F32)] * 2,
        in_specs=[whole] * 5,
        out_specs=[whole] * 2,
        scratch_shapes=[
            pltpu.VMEM((DET, LINE * K, SAMP), BF16),
            pltpu.VMEM((DET, LANES, SAMP), BF16),
            pltpu.VMEM((256, LINE * LISTS_HERE * K), BF16),
            pltpu.VMEM((256, 256), F32),
            pltpu.VMEM((4, DET, SAMP), F32),
            pltpu.VMEM((64, LANES), F32),
            pltpu.VMEM((3 * LANES, 256), BF16),
            pltpu.VMEM((DET, SAMP), F32),
            pltpu.VMEM((DET, SAMP), F32),
            pltpu.VMEM((OUT, PLANE, 8, LANES), F32),
            pltpu.VMEM((OUT, PLANE, 8, LANES), F32),
            pltpu.VMEM((OUT, 2, LINE, 1, LANES), F32),
            pltpu.VMEM((OUT, 2, LINE, 1, LANES), F32),
            pltpu.VMEM((BACK, 2, LINE, 1, LANES), F32),
            pltpu.VMEM((BACK, 2, LINE, 1, LANES), F32),
            pltpu.VMEM((BACK, 64, LANES), F32),
            pltpu.VMEM((BACK, PLANE, 8, LANES), F32),
            pltpu.VMEM((ITERS, 1, LANES), F32),
            pltpu.VMEM((ITERS, LINE, 1, LANES), F32),
            pltpu.VMEM((ITERS, 1, LANES), F32),
            pltpu.VMEM((ITERS, PLANE, 1, LANES), F32),
        ]
        + [dma((OUT,))] * 4 + [dma((BACK,))] * 4 + [dma((ITERS,))] * 4,
        compiler_params=pltpu.CompilerParams(
            collective_id=0, has_side_effects=True, vmem_limit_bytes=40 * 1024 * 1024
        ),
    )(ids, tod, sample_slot, sample_offset, prior)


def solution(mesh):
    rows = P(("grp", "blk", "rep"), None)
    return jax.shard_map(
        shards,
        mesh=mesh,
        in_specs=(rows, P(("grp", "blk"), None, None), rows, rows, rows),
        out_specs=(rows, rows),
        check_vma=False,
    )
```

```python
import functools
import math

import jax
import jax.numpy as jnp
from jax import lax
from jax.experimental import pallas as pl
from jax.experimental.pallas import tpu as pltpu
from jax.sharding import PartitionSpec as P

BL = 64
K = 8
LISTS_HERE = 8
REPS = 4
PLANE = 32
LINE = 32
SHARE = 4
DET = 8
SAMP = 1024
LANES = 128
BASES = 16
TILES = SAMP // LANES
ITERS = 3
COPIES = 2
WINDOW = LINE // COPIES
ROWS = 2 * COPIES
F32 = jnp.float32
BF16 = jnp.bfloat16
MESH = pl.DeviceIdType.MESH

ROUNDS = 1 + ITERS
HITS = ROUNDS
OUT = ROUNDS + 1


def pieces(value, count):
    parts = []
    for _ in range(count):
        part = value.astype(BF16)
        value = value - part.astype(F32)
        parts.append(part)
    return parts


def lanes_of(shape):
    return lax.broadcasted_iota(jnp.int32, shape, len(shape) - 1)


def kernel(
    ids_in, tod_in, slot_in, off_in, prior_in, x_ref, r_ref,
    ids_ref, tod_ref, slot_ref, off_ref, prior_ref, in_sem,
    idsend, idz, idq, idp, id_sem, iterate, residual, direction, along, rest, held, divisor, rr_ref, step_ref,
    s_hot, o_hot, id_hot, near_hot, acc, part, tmp, mt, yrow,
    psend, prec, zsend, zrec, bsend, brec, csend, crec, ssend, srec, tsend, trec, wsend, wrec, usend, urec,
    ps_sem, pr_sem, zs_sem, zr_sem, bs_sem, br_sem, cs_sem, cr_sem,
    ss_sem, sr_sem, ts_sem, tr_sem, ws_sem, wr_sem, us_sem, ur_sem,
):
    grp = lax.axis_index("grp")
    blk = lax.axis_index("blk")
    rep = lax.axis_index("rep")
    me = grp * REPS + rep
    chips = LISTS_HERE // 2

    def farthest_first(i, size):
        return size // 2 + (1 - 2 * (i % 2)) * ((i + 1) // 2)

    def plane_peer(i):
        dx, dc, dy = i // (2 * REPS), (i // REPS) % 2, i % REPS
        g = ((grp // 2 + dx) % chips) * 2 + (grp % 2 + dc) % 2
        return g, (rep + dy) % REPS

    def line_peer(i):
        return (blk + farthest_first(i, LINE)) % LINE

    def near_step(i):
        step = (WINDOW // 2 - (i + 1) // 2) * (2 * (i % 2) - 1)
        return step

    def plane_send(source, target, send, recv):
        @pl.loop(1, PLANE)
        def _(i):
            g, y = plane_peer(i)
            pltpu.make_async_remote_copy(
                src_ref=source(g, y), dst_ref=target, send_sem=send, recv_sem=recv,
                device_id={"grp": g, "rep": y}, device_id_type=MESH,
            ).start()

    def line_send(source, target, send, recv):
        @pl.loop(0, LINE - 1)
        def _(i):
            z = line_peer(i)
            pltpu.make_async_remote_copy(
                src_ref=source(z), dst_ref=target(z), send_sem=send, recv_sem=recv,
                device_id={"blk": z}, device_id_type=MESH,
            ).start()

    def near_send(source, target, send, recv):
        @pl.loop(0, WINDOW - 1)
        def _(i):
            step = near_step(i)
            pltpu.make_async_remote_copy(
                src_ref=source(step), dst_ref=target, send_sem=send, recv_sem=recv,
                device_id={"blk": (blk + step + LINE) % LINE}, device_id_type=MESH,
            ).start()

    def arrived(view, sem):
        pltpu.make_async_copy(view, view, sem).wait()

    barrier = pltpu.get_barrier_semaphore()
    inputs = [
        pltpu.make_async_copy(source, target, in_sem.at[i])
        for i, (source, target) in enumerate(
            [(slot_in, slot_ref), (off_in, off_ref), (tod_in, tod_ref),
             (ids_in, ids_ref), (prior_in, prior_ref)]
        )
    ]
    for copy in inputs:
        copy.start()

    @pl.loop(1, PLANE)
    def _(i):
        g, y = plane_peer(i)
        pl.semaphore_signal(barrier, inc=1, device_id={"grp": g, "rep": y}, device_id_type=MESH)

    @pl.loop(0, LINE - 1)
    def _(i):
        pl.semaphore_signal(
            barrier, inc=1, device_id={"blk": line_peer(i)}, device_id_type=MESH
        )

    for copy in inputs:
        copy.wait()

    @pl.loop(0, DET)
    def _(d):
        slot = slot_ref[pl.ds(d, 1), :]
        owner = slot // K
        place = (slot % K) * LINE + (owner % WINDOW) * COPIES + owner // WINDOW
        rows = lax.broadcasted_iota(jnp.int32, (LINE * K, SAMP), 0)
        s_hot[d] = jnp.where(rows == place, 1.0, 0.0).astype(BF16)
        rows = lax.broadcasted_iota(jnp.int32, (LANES, SAMP), 0)
        o_hot[d] = jnp.where(rows == off_ref[pl.ds(d, 1), :], 1.0, 0.0).astype(BF16)

    def local_map(first):
        acc[...] = jnp.zeros_like(acc)
        for d in range(DET):
            hot = o_hot[d]
            left = []
            for p in (first, first + 1):
                row = part[p, d : d + 1, :]
                left.append(hot * jnp.broadcast_to(row, (LANES, SAMP)).astype(BF16))
            acc[...] += lax.dot_general(
                jnp.concatenate(left, axis=0), s_hot[d],
                (((1,), (1,)), ((), ())), preferred_element_type=F32,
            )

    def send_map(f, image):
        for g in range(PLANE):
            for kh in range(2):
                psend[f, g, kh * SHARE : (kh + 1) * SHARE, :] = image[
                    g * SHARE : (g + 1) * SHARE, kh * LANES : (kh + 1) * LANES
                ]
        prec[f, me] = psend[f, me]
        plane_send(
            lambda g, y: psend.at[f, g * REPS + y], prec.at[f, me], ps_sem.at[f], pr_sem.at[f]
        )

    def to_owners(f):
        arrived(prec.at[f, pl.ds(0, PLANE - 1)], pr_sem.at[f])
        for l in range(LISTS_HERE):
            total = prec[f, l * REPS]
            for y in range(1, REPS):
                total = total + prec[f, l * REPS + y]
            tmp[0, l * 8 : l * 8 + 8, :] = total
        half = [
            [tmp[0, pl.ds(kh * SHARE + j, 8, stride=8), :] for kh in range(2)]
            for j in range(SHARE)
        ]
        lane = lanes_of((8, LANES))
        groups = []
        for kqh in range(2):
            for j in range(SHARE):
                for kql in range(2):
                    kq = kqh * 2 + kql
                    low = pltpu.roll(half[j][0], (-32 * kq) % LANES, 1)
                    high = pltpu.roll(half[j][1], (32 - 32 * kq) % LANES, 1)
                    groups.append(jnp.where(lane < 32, low, high))
        turned = jnp.transpose(jnp.concatenate(groups, axis=0))
        for w in range(WINDOW):
            for kh in range(2):
                start = kh * LINE + w * COPIES
                zsend[f, w, kh * COPIES : (kh + 1) * COPIES, :] = turned[start : start + COPIES]
        zrec[f, LINE // 2] = zsend[f, blk % WINDOW]
        line_send(
            lambda z: zsend.at[f, z % WINDOW],
            lambda z: zrec.at[f, line_slot(z)],
            zs_sem.at[f], zr_sem.at[f],
        )

    def line_slot(z):
        return (blk - z + LINE + LINE // 2) % LINE

    def at_owner(f, copy):
        rows = jnp.concatenate(
            [zrec[f, :, kh * COPIES + copy, :] for kh in range(2)], axis=0
        )
        both = jnp.concatenate([rows, pltpu.roll(rows, 64, 1)], axis=0)
        tmp[copy] = jnp.transpose(both)[:64]
        return jnp.concatenate(
            [tmp[copy, pl.ds(b, SHARE, stride=16), :] for b in range(16)], axis=1
        )

    def merged(f, count):
        arrived(zrec.at[f, pl.ds(0, LINE - 1)], zr_sem.at[f])
        totals = []
        for copy in range(COPIES):
            left = jnp.concatenate(pieces(at_owner(f, copy), count), axis=0)
            out = lax.dot_general(
                left, id_hot[copy], (((1,), (1,)), ((), ())), preferred_element_type=F32
            )
            total = out[:SHARE]
            for p in range(1, count):
                total = total + out[p * SHARE : (p + 1) * SHARE]
            totals.append(total)
        return jnp.concatenate(totals, axis=0)

    def near_lanes(shape):
        lane = lanes_of(shape)
        return lane // 64, (lane // ROWS) % WINDOW, (lane // COPIES) % 2, lane % COPIES

    def hot_ids():
        half, place, kh, copies = near_lanes((LANES, LANES))
        place = half * 64 + kh * LINE + LINE // 2 - WINDOW // 2 + place
        source = lax.broadcasted_iota(jnp.int32, (LANES, LANES), 0)
        near = jnp.zeros((16, LANES), F32)
        rows = lax.broadcasted_iota(jnp.int32, (256, LANES), 0)
        for copy in range(COPIES):
            ids = jnp.concatenate([idp[:, copy * 2 + kql, :] for kql in range(2)], axis=0)
            pick = jnp.where((source == place) & (copies == copy), 1.0, 0.0).astype(BF16)
            near = near + jnp.dot(ids.astype(BF16), pick, preferred_element_type=F32)
            ids = ids.astype(jnp.int32)
            for b in range(16):
                id_hot[copy, :, b * LANES : (b + 1) * LANES] = jnp.where(
                    rows == ids[b : b + 1], 1.0, 0.0
                ).astype(BF16)
        near = near.astype(jnp.int32)
        for b in range(16):
            near_hot[:, b * LANES : (b + 1) * LANES] = jnp.where(
                rows == near[b : b + 1], 1.0, 0.0
            ).astype(BF16)

    def send_back(b, values, count):
        left = jnp.concatenate(pieces(values, count), axis=0)
        out = jnp.dot(left, near_hot[...], preferred_element_type=F32)
        total = out[: COPIES * SHARE]
        for p in range(1, count):
            total = total + out[p * COPIES * SHARE : (p + 1) * COPIES * SHARE]
        copies = near_lanes((SHARE, LANES))[3]
        for c in range(16):
            chunk = total[:, c * LANES : (c + 1) * LANES]
            mine = chunk[:SHARE]
            for copy in range(1, COPIES):
                mine = jnp.where(copies == copy, chunk[copy * SHARE : (copy + 1) * SHARE], mine)
            tmp[0, pl.ds(c, SHARE, stride=16), :] = mine
        turned = jnp.transpose(
            jnp.concatenate([tmp[0], jnp.zeros((64, LANES), F32)], axis=0)
        )
        rows = jnp.where(
            lanes_of((64, LANES)) < 64, turned[:64], pltpu.roll(turned[64:], 64, 1)
        )
        for w in range(WINDOW):
            bsend[b, w] = rows[w * ROWS : (w + 1) * ROWS]
        brec[b, blk % WINDOW] = bsend[b, WINDOW // 2]
        near_send(
            lambda step: bsend.at[b, step + WINDOW // 2], brec.at[b, blk % WINDOW],
            bs_sem.at[b], br_sem.at[b],
        )

    def to_lists(b):
        arrived(brec.at[b, pl.ds(0, WINDOW - 1)], br_sem.at[b])
        rows = jnp.concatenate(
            [
                brec[b, w, kh * COPIES : (kh + 1) * COPIES, :]
                for kh in range(2)
                for w in range(WINDOW)
            ],
            axis=0,
        )
        turned = jnp.transpose(
            jnp.concatenate([rows, jnp.zeros((64, LANES), F32)], axis=0)
        )
        quarter = lanes_of((8, LANES)) // 32
        for j in range(SHARE):
            for kh in range(2):
                tile = jnp.zeros((8, LANES), F32)
                for kq in range(4):
                    start = (kq // 2) * 64 + j * 16 + (kq % 2) * 8
                    moved = pltpu.roll(
                        turned[start : start + 8], (32 * kq - 32 * kh) % LANES, 1
                    )
                    tile = jnp.where(quarter == kq, moved, tile)
                csend[b, pl.ds(kh * SHARE + j, 8, stride=8), :] = tile
        crec[b, me] = csend[b, pl.ds(pl.multiple_of(grp * 8, 8), 8), :]
        plane_send(
            lambda g, y: csend.at[b, pl.ds(pl.multiple_of(g * 8, 8), 8)],
            crec.at[b, me], cs_sem.at[b], cr_sem.at[b],
        )

    def picked(b, passes):
        arrived(crec.at[b, pl.ds(0, PLANE - 1)], cr_sem.at[b])
        for kh in range(2):
            for g in range(0, PLANE, 2):
                at = slice(kh * SHARE, (kh + 1) * SHARE)
                rows = jnp.concatenate([crec[b, g, at, :], crec[b, g + 1, at, :]], axis=0)
                acc[g * SHARE : g * SHARE + 8, kh * LANES : (kh + 1) * LANES] = rows
        for p, piece in enumerate(pieces(acc[:LANES, :], 3)):
            mt[p * LANES : (p + 1) * LANES, :] = piece
        yrow[...] = jnp.zeros_like(yrow)

        @pl.loop(0, passes)
        def _(q):
            left = mt[pl.ds(pl.multiple_of(q * 2 * LANES, 2 * LANES), 2 * LANES), :]
            for d in range(DET):
                out = jnp.dot(left, s_hot[d], preferred_element_type=F32)
                total = out[:LANES] + out[LANES:]
                yrow[d : d + 1, :] += jnp.sum(
                    total * o_hot[d].astype(F32), axis=0, keepdims=True
                )

        return folded(yrow[...])

    def tiles(value):
        return [value[:, t * LANES : (t + 1) * LANES] for t in range(TILES)]

    def folded(value):
        stacked = jnp.concatenate(tiles(value), axis=0)
        a = lax.broadcasted_iota(jnp.int32, (LANES, LANES), 0) // BL
        b = lanes_of((LANES, LANES)) // BL
        ones = jnp.where(a == b, 1.0, 0.0).astype(BF16)
        left = jnp.concatenate(pieces(stacked, 3), axis=0)
        out = jnp.dot(left, ones, preferred_element_type=F32)
        out = out[:64] + out[64:128] + out[128:]
        return jnp.concatenate([out[t * 8 : t * 8 + 8] for t in range(TILES)], axis=1)

    def smoothed(value):
        here = tiles(value)
        swapped = [pltpu.roll(t, 64, 1) for t in here]
        low = lanes_of((DET, LANES)) < 64
        odd = [jnp.where(low, swapped[t - 1], swapped[t]) for t in range(TILES)]
        spectrum = [
            jnp.broadcast_to(prior_ref[:, f : f + 1], (DET, LANES)) for f in range(BASES // 2 + 1)
        ]
        out = [jnp.zeros((DET, LANES), F32) for _ in range(TILES)]
        for shift in range(BASES):
            weight = jnp.zeros((DET, LANES), F32)
            for f in range(BASES // 2 + 1):
                share = (1.0 if f in (0, BASES // 2) else 2.0) / BASES
                weight = weight + spectrum[f] * (
                    share * math.cos(2.0 * math.pi * ((f * shift) % BASES) / BASES)
                )
            source = odd if shift % 2 else here
            for t in range(TILES):
                out[t] = out[t] + weight * source[(t - shift // 2) % TILES]
        return jnp.concatenate(out, axis=1)

    def lane_sums(value):
        total = functools.reduce(lambda a, b: a + b, tiles(value))
        total = jnp.sum(total, axis=0, keepdims=True)
        return total + pltpu.roll(total, 64, 1)

    rank = lax.broadcasted_iota(jnp.int32, (WINDOW, LINE), 0)
    owner = lanes_of((WINDOW, LINE))
    entry, lane = lax.broadcasted_iota(jnp.int32, (K, LANES), 0), lanes_of((K, LANES))
    listed = ids_ref[0].astype(F32).astype(BF16)
    row = jnp.zeros((WINDOW, LANES), F32)
    for copy in range(COPIES):
        pick = jnp.where(owner == copy * WINDOW + rank, 1.0, 0.0).astype(BF16)
        taken = jnp.dot(pick, listed, preferred_element_type=F32)
        pick = jnp.where(lane == copy * K + entry, 1.0, 0.0).astype(BF16)
        row = row + jnp.dot(taken.astype(BF16), pick, preferred_element_type=F32)
    idsend[...] = row.reshape(WINDOW, 1, LANES)

    def send_ids():
        idz[LINE // 2] = idsend[blk % WINDOW]
        line_send(
            lambda z: idsend.at[z % WINDOW], lambda z: idz.at[line_slot(z)],
            id_sem.at[0], id_sem.at[1],
        )

    def share_ids():
        arrived(idz.at[pl.ds(0, LINE - 1)], id_sem.at[1])
        rows = jnp.concatenate(
            [idz[...].reshape(LINE, LANES), jnp.zeros((LANES - LINE, LANES), F32)], axis=0
        )
        turned = jnp.transpose(rows)[: COPIES * K]
        quarter = lanes_of((4, LANES)) // LINE
        mine = jnp.zeros((4, LANES), F32)
        for kqh in range(2):
            for kh in range(2):
                some = [
                    turned[at : at + 1]
                    for copy in range(COPIES)
                    for kql in range(2)
                    for at in [copy * K + kh * 4 + kqh * 2 + kql]
                ]
                place = kqh * 2 + kh
                moved = pltpu.roll(jnp.concatenate(some, axis=0), place * LINE, 1)
                mine = jnp.where(quarter == place, moved, mine)
        idq[...] = mine
        idp[grp] = mine

        @pl.loop(1, LISTS_HERE)
        def _(i):
            g = ((grp // 2 + i // 2) % chips) * 2 + (grp % 2 + i % 2) % 2
            pltpu.make_async_remote_copy(
                src_ref=idq, dst_ref=idp.at[grp], send_sem=id_sem.at[2], recv_sem=id_sem.at[3],
                device_id={"grp": g}, device_id_type=MESH,
            ).start()

        arrived(idp.at[pl.ds(0, LISTS_HERE - 1)], id_sem.at[3])

    for p, piece in enumerate(pieces(tod_ref[...], 3)):
        part[p] = piece.astype(F32)
    part[3] = jnp.ones((DET, SAMP), F32)
    mt[3 * LANES :, :] = jnp.zeros((LANES, 256), BF16)
    for ref in (iterate, residual, direction, along):
        ref[...] = jnp.zeros_like(ref)
    for ref in (rr_ref, step_ref):
        ref[...] = jnp.ones_like(ref)
    low = lanes_of((1, LANES)) < 64

    @pl.loop(0, ROUNDS)
    def _(n):
        passes = jnp.where(n == 0, 2, 1)

        @pl.loop(0, passes)
        def _(q):
            local_map(2 * q)

            @pl.when(q == 0)
            def _():
                held[...] = acc[:LANES, :] + acc[LANES:, :]

            @pl.when(q == 1)
            def _():
                held[...] += acc[:LANES, :]

        @pl.when(n == 0)
        def _():
            pl.semaphore_wait(barrier, PLANE + LINE - 2)

        send_map(n, held[...])

        @pl.when(n == 0)
        def _():
            send_map(HITS, acc[LANES:, :])
            send_ids()
            rest[...] = folded(tod_ref[...])

        @pl.when(n > 0)
        def _():
            value = residual[...]
            image = BL * value + smoothed(value)
            rest[...] = image
            square = lane_sums(value * value) * (1.0 / BL)
            product = lane_sums(value * image) * (1.0 / BL)
            row = jnp.where(low, square, product)
            ssend[n] = row
            srec[n, me] = row
            plane_send(lambda g, y: ssend.at[n], srec.at[n, me], ss_sem.at[n], sr_sem.at[n])

        to_owners(n)

        @pl.when(n == 0)
        def _():
            to_owners(HITS)
            share_ids()
            hot_ids()
            divisor[...] = jnp.maximum(merged(HITS, 3), 1.0)

        @pl.when(n > 0)
        def _():
            arrived(srec.at[n, pl.ds(0, PLANE - 1)], sr_sem.at[n])
            row = jnp.sum(srec[n], axis=0)
            tsend[n] = row
            trec[n, blk] = row
            line_send(
                lambda z: tsend.at[n], lambda z: trec.at[n, blk], ts_sem.at[n], tr_sem.at[n]
            )

        sums = merged(n, 3)
        binned = sums / divisor[...]
        send_back(n, binned, 3)

        @pl.when(n > 0)
        def _():
            energy = jnp.sum(sums * binned, axis=0, keepdims=True)
            row = energy[:, :LANES] + energy[:, LANES:]
            wsend[n] = row
            wrec[n, blk % WINDOW] = row
            near_send(
                lambda step: wsend.at[n], wrec.at[n, blk % WINDOW], ws_sem.at[n], wr_sem.at[n]
            )

        to_lists(n)

        @pl.when(n > 0)
        def _():
            arrived(wrec.at[n, pl.ds(0, WINDOW - 1)], wr_sem.at[n])
            row = jnp.sum(wrec[n], axis=0)
            usend[n] = row
            urec[n, me] = row
            plane_send(lambda g, y: usend.at[n], urec.at[n, me], us_sem.at[n], ur_sem.at[n])

        image = rest[...] - picked(n, passes)

        @pl.when(n == 0)
        def _():
            residual[...] = image

        @pl.when(n > 0)
        def _():
            arrived(trec.at[n, pl.ds(0, LINE - 1)], tr_sem.at[n])
            arrived(urec.at[n, pl.ds(0, PLANE - 1)], ur_sem.at[n])
            row = jnp.sum(trec[n], axis=0)
            energy = jnp.sum(jnp.sum(urec[n], axis=0), axis=1, keepdims=True)
            new = jnp.sum(jnp.where(low, row, 0.0), axis=1, keepdims=True)
            curve = jnp.sum(jnp.where(low, 0.0, row), axis=1, keepdims=True) - energy
            ratio = jnp.where(n == 1, 0.0, new / rr_ref[:, 0:1])
            step = new / (curve - ratio * new / step_ref[:, 0:1])
            rr_ref[...] = jnp.broadcast_to(new, (1, LANES))
            step_ref[...] = jnp.broadcast_to(step, (1, LANES))
            course = residual[...] + ratio * direction[...]
            change = image + ratio * along[...]
            direction[...] = course
            along[...] = change
            iterate[...] += step * course
            residual[...] -= step * change

        for p, piece in enumerate(pieces(residual[...], 2)):
            part[p] = piece.astype(F32)

    for ref, value in ((x_ref, iterate[...]), (r_ref, residual[...])):
        out = jnp.zeros((DET, LANES), F32)
        lane = lanes_of((DET, LANES))
        for t, tile in enumerate(tiles(value)):
            for side in range(2):
                spread = jnp.broadcast_to(tile[:, side * BL : side * BL + 1], (DET, LANES))
                out = jnp.where(lane == 2 * t + side, spread, out)
        ref[...] = out[:, :BASES]

    arrived(idz.at[pl.ds(0, LINE - 1)], id_sem.at[0])
    arrived(idp.at[pl.ds(0, LISTS_HERE - 1)], id_sem.at[2])
    for f in range(OUT):
        arrived(prec.at[f, pl.ds(0, PLANE - 1)], ps_sem.at[f])
        arrived(zrec.at[f, pl.ds(0, LINE - 1)], zs_sem.at[f])
    for b in range(ROUNDS):
        arrived(brec.at[b, pl.ds(0, WINDOW - 1)], bs_sem.at[b])
        arrived(crec.at[b, pl.ds(0, PLANE - 1)], cs_sem.at[b])
    for n in range(1, ROUNDS):
        arrived(srec.at[n, pl.ds(0, PLANE - 1)], ss_sem.at[n])
        arrived(trec.at[n, pl.ds(0, LINE - 1)], ts_sem.at[n])
        arrived(wrec.at[n, pl.ds(0, WINDOW - 1)], ws_sem.at[n])
        arrived(urec.at[n, pl.ds(0, PLANE - 1)], us_sem.at[n])


def shards(tod, hit_ids, sample_slot, sample_offset, prior):
    whole = pl.BlockSpec(memory_space=pltpu.VMEM)
    dma = pltpu.SemaphoreType.DMA
    return pl.pallas_call(
        kernel,
        out_shape=[jax.ShapeDtypeStruct((DET, BASES), F32)] * 2,
        in_specs=[pl.BlockSpec(memory_space=pl.ANY)] * 5,
        out_specs=[whole] * 2,
        scratch_shapes=[
            pltpu.VMEM((1, LINE, K), jnp.int32),
            pltpu.VMEM((DET, SAMP), F32),
            pltpu.VMEM((DET, SAMP), jnp.int32),
            pltpu.VMEM((DET, SAMP), jnp.int32),
            pltpu.VMEM((DET, BASES // 2 + 1), F32),
            dma((5,)),
            pltpu.VMEM((WINDOW, 1, LANES), F32),
            pltpu.VMEM((LINE, 1, LANES), F32),
            pltpu.VMEM((4, LANES), F32),
            pltpu.VMEM((LISTS_HERE, 4, LANES), F32),
            dma((4,)),
            pltpu.VMEM((DET, SAMP), F32),
            pltpu.VMEM((DET, SAMP), F32),
            pltpu.VMEM((DET, SAMP), F32),
            pltpu.VMEM((DET, SAMP), F32),
            pltpu.VMEM((DET, SAMP), F32),
            pltpu.VMEM((LANES, 256), F32),
            pltpu.VMEM((COPIES * SHARE, 256), F32),
            pltpu.VMEM((1, LANES), F32),
            pltpu.VMEM((1, LANES), F32),
            pltpu.VMEM((DET, LINE * K, SAMP), BF16),
            pltpu.VMEM((DET, LANES, SAMP), BF16),
            pltpu.VMEM((COPIES, 256, LINE * LISTS_HERE * K), BF16),
            pltpu.VMEM((256, LINE * LISTS_HERE * K), BF16),
            pltpu.VMEM((256, 256), F32),
            pltpu.VMEM((4, DET, SAMP), F32),
            pltpu.VMEM((COPIES, 64, LANES), F32),
            pltpu.VMEM((4 * LANES, 256), BF16),
            pltpu.VMEM((DET, SAMP), F32),
            pltpu.VMEM((OUT, PLANE, 8, LANES), F32),
            pltpu.VMEM((OUT, PLANE, 8, LANES), F32),
            pltpu.VMEM((OUT, WINDOW, ROWS, LANES), F32),
            pltpu.VMEM((OUT, LINE, ROWS, LANES), F32),
            pltpu.VMEM((ROUNDS, WINDOW, ROWS, LANES), F32),
            pltpu.VMEM((ROUNDS, WINDOW, ROWS, LANES), F32),
            pltpu.VMEM((ROUNDS, 64, LANES), F32),
            pltpu.VMEM((ROUNDS, PLANE, 8, LANES), F32),
            pltpu.VMEM((ROUNDS, 1, LANES), F32),
            pltpu.VMEM((ROUNDS, PLANE, 1, LANES), F32),
            pltpu.VMEM((ROUNDS, 1, LANES), F32),
            pltpu.VMEM((ROUNDS, LINE, 1, LANES), F32),
            pltpu.VMEM((ROUNDS, 1, LANES), F32),
            pltpu.VMEM((ROUNDS, WINDOW, 1, LANES), F32),
            pltpu.VMEM((ROUNDS, 1, LANES), F32),
            pltpu.VMEM((ROUNDS, PLANE, 1, LANES), F32),
        ]
        + [dma((OUT,))] * 4 + [dma((ROUNDS,))] * 4 + [dma((ROUNDS,))] * 8,
        compiler_params=pltpu.CompilerParams(
            collective_id=0, has_side_effects=True, vmem_limit_bytes=40 * 1024 * 1024
        ),
    )(hit_ids, tod, sample_slot, sample_offset, prior)


def solution(mesh):
    rows = P(("grp", "blk", "rep"), None)
    return jax.shard_map(
        shards,
        mesh=mesh,
        in_specs=(rows, P(("grp", "blk"), None, None), rows, rows, rows),
        out_specs=(rows, rows),
        check_vma=False,
    )
```
